128 devices in a mesh: dp: 8 (over x, z_hi), graph: 16 (over z_lo, y, core).
Axes of the slice: x: 4, y: 4, z: 4 (z_hi: 2, z_lo: 2; z = z_hi * 2 + z_lo), core: 2. Of those that a mesh axis runs over, the one named last changes fastest.
Arguments:
- node_feat: bfloat16 [8, 256, 6272], P('dp', 'graph'), may hold values from -6 to 6
- atomic: int32 [8, 256], P('dp', 'graph'), may hold values from 0 to 89
- edge_src: int32 [8, 4096], P('dp', 'graph'), may hold values from 0 to 255
- edge_dst: int32 [8, 4096], P('dp', 'graph'), may hold values from 0 to 255, as said below
- edge_count: int32 [8, 16], P('dp', 'graph'), may hold values from 64 to 256, as said below
- radial: bfloat16 [8, 4096, 512], P('dp', 'graph'), may hold values from -6 to 6
- species_gain: float32 [90, 896], replicated, may hold values from 0.5 to 2
- w_rad: bfloat16 [512, 896], replicated, may hold values from -0.25 to 0.25
- w_mix: bfloat16 [7, 128, 128], replicated, may hold values from -0.5 to 0.5
- w_out: bfloat16 [7, 128, 128], replicated, may hold values from -0.5 to 0.5
- g_out: bfloat16 [8, 256, 6272], P('dp', 'graph'), may hold values from -6 to 6
Outputs:
- block_out: bfloat16 [8, 256, 6272], P('dp', 'graph')
- node_grad: bfloat16 [8, 256, 6272], P('dp', 'graph')
- edge_grad: bfloat16 [8, 4096, 512], P('dp', 'graph')
- w_mix_grad: float32 [7, 128, 128], replicated
- w_out_grad: float32 [7, 128, 128], replicated
- w_rad_grad: float32 [512, 896], replicated
The draws below stay inside these ranges and needn't reach their ends.
Inputs may be any that keep to these rules, and one draw needn't show every extreme that they name: `edge_count`: in every cell one block of slots is full and the others hold at least a quarter of 256 live slots. `edge_dst`: the destination of slot j of a cell lies among atoms g * 16 to (g + 1) * 16 - 1, where g = (j mod 256) mod 16.
All inputs are finite; a program needn't handle non-finite values.
Results may differ from the reference program's by a relative error of at most 0.019.
Values may be sent and summed in bfloat16 or wider, within the bound.
A program may use at most 128 MiB of HBM per device.

```python
import math
import jax
import jax.numpy as jnp
import numpy as np
from jax import lax

C = 128
LMAX = 6
SPECIES = 90
RB = 512
ATOM_DEV = 16
EDGE_DEV = 256
K = 49
CELLS = 8
ATOMS = 256
EDGES = 4096
N_GRAPH = 16


def draw_edge_count(key, part):
    key = jax.random.fold_in(key, 7)
    first, second = jax.random.split(key)
    counts = jax.random.randint(first, (CELLS, N_GRAPH), EDGE_DEV // 4, EDGE_DEV + 1)
    fullest = jax.random.randint(second, (CELLS,), 0, N_GRAPH)
    marks = jnp.arange(N_GRAPH, dtype=jnp.int32)[None, :] == fullest[:, None]
    return jnp.where(marks, EDGE_DEV, counts).astype(jnp.int32)


def draw_edge_dst(key, part):
    key = jax.random.fold_in(key, 11)
    slots = jnp.arange(EDGES, dtype=jnp.int32)
    owner = slots % EDGE_DEV % N_GRAPH
    offset = jax.random.randint(key, (CELLS, EDGES), 0, ATOM_DEV)
    return (owner[None, :] * ATOM_DEV + offset).astype(jnp.int32)


def set_ends(values, rng, least, top_value):
    index_at = [jax.random.randint(jax.random.fold_in(rng, axis), (), 0, length) for axis, length in enumerate(values.shape)]
    main_axis = values.shape.index(max(values.shape))
    neighbour = index_at[:main_axis] + [(index_at[main_axis] + 1) % values.shape[main_axis]] + index_at[main_axis + 1:]
    return values.at[tuple(index_at)].set(least).at[tuple(neighbour)].set(top_value)


def shard_levels(own_key, dims, shards, least, largest):
    level = 1.0
    for position, shards_of in shards:
        steps = jax.random.uniform(jax.random.fold_in(jax.random.fold_in(own_key, 6), position), (shards_of,), jnp.float32, least / len(shards), largest / len(shards))
        level = level * jnp.repeat(jnp.exp(steps), dims[position] // shards_of).reshape((-1,) + (1,) * (len(dims) - 1 - position))
    return level


def gaussian(key, extent, deviation, reach, cuts=(), held_as=jnp.bfloat16):
    gain = shard_levels(key, extent, cuts, -0.22, 0.18) if cuts else 1.0
    entries = jax.random.normal(key, extent, jnp.float32) * deviation * gain
    return jnp.minimum(jnp.maximum(entries, -reach), reach).astype(held_as)


def setup_inputs(seed: int = 0) -> dict:
    key_list = jax.random.split(jax.random.key(seed), 12)
    node_feat = gaussian(key_list[0], (CELLS, ATOMS, K * C), 1.0, 6.0, ((0, 8), (1, 16)))
    atomic = set_ends(jax.random.randint(key_list[1], (CELLS, ATOMS), 0, SPECIES), jax.random.fold_in(key_list[1], 1), 0, SPECIES - 1).astype(jnp.int32)
    edge_src = set_ends(jax.random.randint(key_list[2], (CELLS, EDGES), 0, ATOMS), jax.random.fold_in(key_list[2], 1), 0, ATOMS - 1).astype(jnp.int32)
    edge_dst = draw_edge_dst(jax.random.fold_in(key_list[11], 71), 0)
    edge_count = draw_edge_count(jax.random.fold_in(key_list[11], 71), 0)
    radial = gaussian(key_list[5], (CELLS, EDGES, RB), 1.0, 6.0, ((0, 8), (1, 16)))
    species_gain = jnp.clip(jnp.exp(jax.random.uniform(key_list[6], (SPECIES, (LMAX + 1) * C), jnp.float32, math.log(0.5), math.log(2.0))), 0.5, 2.0)
    w_rad = gaussian(key_list[7], (RB, (LMAX + 1) * C), RB ** -0.5, 0.25)
    w_mix = gaussian(key_list[8], (LMAX + 1, C, C), C ** -0.5, 0.5)
    w_out = gaussian(key_list[9], (LMAX + 1, C, C), C ** -0.5, 0.5)
    g_out = gaussian(key_list[10], (CELLS, ATOMS, K * C), 1.0, 6.0, ((0, 8), (1, 16)))
    return {"node_feat": node_feat, "atomic": atomic, "edge_src": edge_src, "edge_dst": edge_dst, "edge_count": edge_count, "radial": radial, "species_gain": species_gain, "w_rad": w_rad, "w_mix": w_mix, "w_out": w_out, "g_out": g_out}


def expand_degrees(scales):
    counts = np.array([2 * l + 1 for l in range(LMAX + 1)])
    return jnp.repeat(scales, counts, axis=1, total_repeat_length=K)


def degree_apply(rows, weights):
    pieces = []
    for l in range(LMAX + 1):
        block = rows[:, l * l:(l + 1) * (l + 1), :].astype(jnp.float32)
        pieces.append(jnp.einsum("ekc,cd->ekd", block, weights[l].astype(jnp.float32)))
    return jnp.concatenate(pieces, axis=1)


def degree_outer(left, right):
    pieces = []
    for l in range(LMAX + 1):
        a_part = left[:, l * l:(l + 1) * (l + 1), :].astype(jnp.float32)
        b_part = right[:, l * l:(l + 1) * (l + 1), :].astype(jnp.float32)
        pieces.append(jnp.einsum("ekc,ekd->cd", a_part, b_part))
    return jnp.stack(pieces, axis=0)


def degree_total(values):
    pieces = []
    for l in range(LMAX + 1):
        pieces.append(jnp.sum(values[:, l * l:(l + 1) * (l + 1), :], axis=1))
    return jnp.stack(pieces, axis=1)


def one_cell(feat, elems, source, target, count, rad, grad_in, species_gain, w_rad, w_mix, w_out):
    slots = jnp.arange(EDGES, dtype=jnp.int32)
    live = ((slots % EDGE_DEV) < jnp.repeat(count, EDGE_DEV)).astype(jnp.float32)
    nodes = feat.reshape(ATOMS, K, C)
    xs = jnp.take(nodes, source, axis=0)
    z_src = jnp.take(elems, source, axis=0)
    onehot = (z_src[:, None] == jnp.arange(SPECIES, dtype=jnp.int32)[None, :]).astype(jnp.float32)
    gain_rows = jnp.dot(onehot, species_gain, precision=lax.Precision.HIGHEST)
    scales = jnp.dot(rad, w_rad, preferred_element_type=jnp.float32) * gain_rows
    scales = scales.reshape(EDGES, LMAX + 1, C)
    full_scales = expand_degrees(scales)
    mixed = degree_apply(xs, w_mix)
    message = (mixed * full_scales * live[:, None, None]).astype(jnp.bfloat16)
    agg = 0.25 * jax.ops.segment_sum(message.astype(jnp.float32), target, ATOMS)
    agg_b = agg.astype(jnp.bfloat16)
    out = (nodes.astype(jnp.float32) + degree_apply(agg_b, w_out)).astype(jnp.bfloat16)
    g_nodes = grad_in.reshape(ATOMS, K, C)
    d_agg = (0.25 * degree_apply(g_nodes, jnp.swapaxes(w_out, 1, 2))).astype(jnp.bfloat16)
    wout_g = degree_outer(agg_b, g_nodes)
    d_msg = jnp.take(d_agg, target, axis=0) * live[:, None, None].astype(jnp.bfloat16)
    d_mixed = (d_msg.astype(jnp.float32) * full_scales).astype(jnp.bfloat16)
    d_scales = degree_total(d_msg.astype(jnp.float32) * mixed)
    wmix_g = degree_outer(xs, d_mixed)
    back = degree_apply(d_mixed, jnp.swapaxes(w_mix, 1, 2))
    node_g = g_nodes.astype(jnp.float32) + jax.ops.segment_sum(back, source, ATOMS)
    d_rad = (d_scales.reshape(EDGES, (LMAX + 1) * C) * gain_rows).astype(jnp.bfloat16)
    wrad_g = jnp.dot(rad.T, d_rad, preferred_element_type=jnp.float32)
    e_grad = jnp.dot(d_rad, w_rad.T, preferred_element_type=jnp.float32).astype(jnp.bfloat16)
    return (out.reshape(ATOMS, K * C), node_g.astype(jnp.bfloat16).reshape(ATOMS, K * C), e_grad, wmix_g, wout_g, wrad_g)


def reference(node_feat, atomic, edge_src, edge_dst, edge_count, radial, species_gain, w_rad, w_mix, w_out, g_out):
    def step(inputs):
        return one_cell(*inputs, species_gain, w_rad, w_mix, w_out)

    outs = lax.map(step, (node_feat, atomic, edge_src, edge_dst, edge_count, radial, g_out))
    block_out, node_grad, edge_grad, wmix_g, wout_g, wrad_g = outs
    return (block_out, node_grad, edge_grad, jnp.sum(wmix_g, axis=0), jnp.sum(wout_g, axis=0), jnp.sum(wrad_g, axis=0))
```

```python
import functools

import jax
import jax.numpy as jnp
from jax import lax
from jax.experimental import pallas as pl
from jax.experimental.pallas import tpu as pltpu
from jax.sharding import PartitionSpec as P

MESH = pl.DeviceIdType.MESH
F32, BF16 = jnp.float32, jnp.bfloat16
C = 128
DEGREES = 7
PART_DEGREES = ((6,), (5,), (4, 1), (2, 3, 0))
SLOT_DEGREE = (6, 5, 4, 1, 2, 3, 0)
SLOT_PART = (0, 1, 2, 2, 3, 3, 3)
SLOT_POS = (0, 0, 0, 1, 0, 1, 2)
PART_SLOTS = (1, 1, 2, 3)
KPART = 13
WPART = KPART * C
CHUNKS = ((0, 4), (4, 4), (8, 5))
PIECE = 336
HALF = 8 * PIECE
ROWS = 2 * HALF
TINY = 48


def _place():
    place = {}
    for q, degrees in enumerate(PART_DEGREES):
        at = 0
        for l in degrees:
            for k in range(l * l, (l + 1) * (l + 1)):
                place[k] = (q, at)
                at += 1
    return place


PLACE = _place()


def ks(l):
    return range(l * l, (l + 1) * (l + 1))


def cols(k, n=1):
    return slice(k * C, (k + n) * C)


def iota(shape, dim):
    return lax.broadcasted_iota(jnp.int32, shape, dim)


def dot(a, b):
    return jnp.dot(a, b, preferred_element_type=F32)


def dot_tn(a, b):
    return lax.dot_general(a, b, (((0,), (0,)), ((), ())), preferred_element_type=F32)


def dot_nt(a, b):
    return lax.dot_general(a, b, (((1,), (1,)), ((), ())), preferred_element_type=F32)


def slot_of_row(e):
    y, q, i = e // 64, (e // 16) % 4, e % 16
    return i * 16 + (q // 2) * 8 + y * 2 + q % 2


def kernel(
    dp,
    nf, at, es, ed, ec, rad, gain, wrad, wmix, wout, go,
    bo, ng, eg, gm, gw, gr,
    hs, hall, ds_, dgall, rs, rall, meta_s, meta, oh, oht, od, odt, msg, dmx, drad, drs, drall,
    ss, srecv, aggs, aggr, radp, gains, wl, sibr, hb, grv, db, drv, fin, ag1, ag2, full,
    sem_ag, sem_rs, sem, send,
):
    d = lax.axis_index("dp")
    g = lax.axis_index("graph")
    chip, core = lax.div(g, 2), lax.rem(g, 2)
    y = lax.rem(chip, 4)
    q = lax.div(g, 8) * 2 + core

    def dev(yy, qq):
        return lax.div(qq, 2) * 8 + yy * 2 + lax.rem(qq, 2)

    def rows(start, n):
        return pl.ds(pl.multiple_of(start, 16), n)

    def remote(src, dst, s, r, **where):
        pltpu.make_async_remote_copy(
            src_ref=src, dst_ref=dst, send_sem=s, recv_sem=r, device_id=where, device_id_type=MESH
        ).start()

    def local(src, dst, r):
        pltpu.make_async_copy(src, dst, r).start()

    def wait(ref, s):
        pltpu.make_async_copy(ref, ref, s).wait()

    PEERS = [(t, u) for t in range(4) for u in range(4) if (t, u) != (0, 0)]

    def peer(t, u):
        return lax.rem(y + t, 4), lax.rem(q + u, 4)

    barrier = pltpu.get_barrier_semaphore()
    for t, u in PEERS:
        pl.semaphore_signal(barrier, inc=1, device_id={"graph": dev(*peer(t, u))}, device_id_type=MESH)
    for t in range(1, dp):
        pl.semaphore_signal(barrier, inc=1, device_id={"dp": lax.rem(d + t, dp)}, device_id_type=MESH)

    lane = iota((1, 256), 1)
    src_row = jnp.broadcast_to(es[...].astype(F32), (16, 256)).astype(BF16)
    dst_row = jnp.broadcast_to((ed[...] - (lane % 16) * 16).astype(F32), (16, 256)).astype(BF16)
    out_lane = iota((256, 512), 1)
    in_slot = iota((256, 512), 0)
    wanted = slot_of_row((out_lane // 128) * 64 + out_lane % 64)
    hit = wanted == in_slot
    first = (out_lane % 128) < 64
    put_src = jnp.where(hit & first, 1.0, 0.0).astype(BF16)
    put_dst = jnp.where(hit & ~first, 1.0, 0.0).astype(BF16)
    meta_lane = iota((16, 512), 1) % 128
    offset = jnp.where(meta_lane >= 64, (meta_lane - 64) // 16 * 16, 0).astype(F32)
    meta_row = (dot(src_row, put_src) + dot(dst_row, put_dst) + offset).astype(BF16)
    for yy in range(4):
        meta_s[yy] = meta_row[:, cols(yy)]

    by_row = slot_of_row(iota((256, 256), 0))
    perm = jnp.where(by_row == iota((256, 256), 1), 1.0, 0.0).astype(BF16)
    radp[...] = dot(perm, rad[...]).astype(BF16)
    live = slot_of_row(iota((256, C), 0)) < ec[...]
    scales = dot(radp[...], wrad[...])
    for slot, l in enumerate(SLOT_DEGREE):
        rs[slot * 256 : (slot + 1) * 256, :] = jnp.where(live, scales[:, cols(l)], 0.0).astype(BF16)

    pl.semaphore_wait(barrier, 15 + dp - 1)

    for t, u in PEERS:
        yy, qq = peer(t, u)
        remote(meta_s.at[yy], meta.at[rows(g * 16, 16)], send.at[0], sem.at[0], graph=dev(yy, qq))
    local(meta_s.at[y], meta.at[rows(g * 16, 16)], sem.at[0])
    for t in range(4):
        yy = lax.rem(y + t, 4)
        for slot in range(7):
            part = SLOT_PART[slot]
            src = rs.at[rows(slot * 256 + yy * 64, 64)]
            pos = SLOT_POS[slot]
            dst = rall.at[pos, rows(g * 64, 64)]
            if t == 0:
                @pl.when(q == part)
                def _():
                    local(src, dst, sem.at[1 + pos])

                @pl.when(q != part)
                def _():
                    remote(src, dst, send.at[1], sem.at[1 + pos], graph=dev(yy, part))
            else:
                remote(src, dst, send.at[1], sem.at[1 + pos], graph=dev(yy, part))

    kind = iota((gain.shape[0], 16), 0) == at[...]
    gains[...] = lax.dot_general(
        jnp.where(kind, 1.0, 0.0), gain[...], (((0,), (0,)), ((), ())),
        precision=lax.Precision.HIGHEST, preferred_element_type=F32,
    )

    def stack(ref, l):
        return jnp.concatenate([ref[:, cols(k)] for k in ks(l)], axis=0)

    def gain_rows(l):
        return jnp.concatenate([gains[:, cols(l)]] * (2 * l + 1), axis=0)

    zeros = jnp.zeros((16, C), BF16)
    for buf in (hs, ds_):
        buf[1, :, cols(11)] = zeros
        buf[1, :, cols(12)] = zeros
        buf[2, :, cols(12)] = zeros
    for l in range(DEGREES):
        h = (dot(stack(nf, l), wmix[l]) * gain_rows(l)).astype(BF16)
        for n, k in enumerate(ks(l)):
            part, pos = PLACE[k]
            hs[part, :, cols(pos)] = h[n * 16 : (n + 1) * 16]
    for c, (at_k, n_k) in enumerate(CHUNKS):
        cs = cols(at_k, n_k)
        for t, u in PEERS:
            yy, qq = peer(t, u)
            remote(hs.at[qq, :, cs], hall.at[rows(g * 16, 16), cs], send.at[2], sem_ag.at[c], graph=dev(yy, qq))
        local(hs.at[q, :, cs], hall.at[rows(g * 16, 16), cs], sem_ag.at[c])

    for l in range(DEGREES):
        dagg = (0.25 * dot_nt(stack(go, l), wout[l])).astype(BF16)
        for n, k in enumerate(ks(l)):
            part, pos = PLACE[k]
            ds_[part, :, cols(pos)] = dagg[n * 16 : (n + 1) * 16]
    for u in range(1, 4):
        qq = lax.rem(q + u, 4)
        remote(ds_.at[qq], dgall.at[rows(q * 16, 16)], send.at[3], sem.at[4], graph=dev(y, qq))
    local(ds_.at[q], dgall.at[rows(q * 16, 16)], sem.at[4])
    dgall[64:128, :] = jnp.zeros((64, WPART), BF16)

    wait(meta, sem.at[0])
    ones = jnp.ones((C, C), BF16)
    for s in range(16):
        block = meta[s * 16 : (s + 1) * 16, :].astype(F32)
        block = jnp.concatenate([block] * 4, axis=0)
        here, ln = iota((64, C), 0), iota((64, C), 1)
        src = dot(jnp.where(ln == here, block, 0.0).astype(BF16), ones)
        dst = dot(jnp.where(ln == here + 64, block, 0.0).astype(BF16), ones)
        lnf = ln.astype(F32)
        rr = slice(s * 64, (s + 1) * 64)
        oh[rr, :C] = jnp.where(src == lnf, 1.0, 0.0).astype(BF16)
        oh[rr, C:] = jnp.where(src == lnf + 128.0, 1.0, 0.0).astype(BF16)
        od[rr, :] = jnp.where(dst == lnf, 1.0, 0.0).astype(BF16)
    oht[...] = oh[...].astype(F32).T.astype(BF16)
    odt[...] = od[...].astype(F32).T.astype(BF16)

    drad[...] = jnp.zeros(drad.shape, F32)
    wait(rall.at[0], sem.at[1])

    @pl.when(q >= 2)
    def _():
        wait(rall.at[1], sem.at[2])

    @pl.when(q == 3)
    def _():
        wait(rall.at[2], sem.at[3])

    wait(dgall.at[0:64], sem.at[4])

    is2 = lax.div(q * (q - 1) * (3 - q), 2)
    is3 = lax.div(q * (q - 1) * (q - 2), 6)

    for c, (at_k, n_k) in enumerate(CHUNKS):
        cs = cols(at_k, n_k)
        wait(hall.at[:, cs], sem_ag.at[c])

        def tile(e, carry):
            er = pl.ds(pl.multiple_of(e * 256, 256), 256)
            hx = dot(oh[er, :], hall[:, cs])
            dm = dot(od[er, :], dgall[:, cs])
            for n in range(n_k):
                k = at_k + n
                pos = is2 * (k // 9) + is3 * ((k + 7) // 12 + k // 12)
                r = rall[pos, er, :].astype(F32)
                h_k, d_k = hx[:, cols(n)], dm[:, cols(n)]
                msg[er, cols(n)] = (h_k * r).astype(BF16)
                dmx[er, cols(n)] = (d_k * r).astype(BF16)
                drad[pos, er, :] += h_k * d_k
            return carry

        lax.fori_loop(0, 4, tile, 0)
        ss[:, cs] = dot(oht[...], dmx[:, : n_k * C]).astype(BF16)
        for t, u in PEERS:
            yy, qq = peer(t, u)
            to = dev(yy, qq)
            remote(ss.at[rows(to * 16, 16), cs], srecv.at[q, y, :, cs], send.at[4], sem_rs.at[c], graph=to)
        local(ss.at[rows(g * 16, 16), cs], srecv.at[q, y, :, cs], sem_rs.at[c])
        aggs[:, cs] = (0.25 * dot(odt[...], msg[:, : n_k * C])[:64]).astype(BF16)
    for u in range(1, 4):
        qq = lax.rem(q + u, 4)
        remote(aggs.at[rows(qq * 16, 16)], aggr.at[q], send.at[5], sem.at[5], graph=dev(y, qq))
    local(aggs.at[rows(q * 16, 16)], aggr.at[q], sem.at[5])

    drs[...] = drad[...].astype(BF16)
    base = q + lax.div(q, 3)
    for n_s, cond in ((1, q < 2), (2, q == 2), (3, q == 3)):
        @pl.when(cond)
        def _():
            for t, u in PEERS:
                to = dev(*peer(t, u))
                remote(
                    drs.at[pl.ds(0, n_s), rows(to * 64, 64)], drall.at[pl.ds(base, n_s), rows(y * 64, 64)],
                    send.at[6], sem.at[6], graph=to,
                )
            local(drs.at[pl.ds(0, n_s), rows(g * 64, 64)], drall.at[pl.ds(base, n_s), rows(y * 64, 64)], sem.at[6])

    def stack_parts(ref, l):
        return jnp.concatenate([ref[PLACE[k][0], :, cols(PLACE[k][1])] for k in ks(l)], axis=0)

    wait(aggr, sem.at[5])
    for l in range(DEGREES):
        agg = stack_parts(aggr, l)
        out = (dot(agg, wout[l]) + stack(nf, l).astype(F32)).astype(BF16)
        for n, k in enumerate(ks(l)):
            bo[:, cols(k)] = out[n * 16 : (n + 1) * 16]
        wl[(DEGREES + l) * C : (DEGREES + l + 1) * C, :] = dot_tn(agg, stack(go, l)).astype(BF16)

    wait(drall, sem.at[6])
    d_rad = []
    for l in range(DEGREES):
        d_rad.append(jnp.where(live, drall[SLOT_DEGREE.index(l)].astype(F32), 0.0).astype(BF16))
    d_rad = jnp.concatenate(d_rad, axis=1)
    w_part = dot_tn(radp[...], d_rad).astype(BF16)
    for l in range(DEGREES):
        at_row = 2 * DEGREES * C + l * 512
        wl[at_row : at_row + 512, :] = w_part[:, cols(l)]
    e_part = dot_nt(d_rad, wrad[...]).astype(BF16)
    back = slot_of_row(iota((256, 256), 1)) == iota((256, 256), 0)
    eg[...] = dot(jnp.where(back, 1.0, 0.0).astype(BF16), e_part).astype(BF16)

    for c, (at_k, n_k) in enumerate(CHUNKS):
        wait(srecv.at[:, :, :, cols(at_k, n_k)], sem_rs.at[c])
    for l in range(DEGREES):
        total = stack_parts(srecv.at[:, 0], l).astype(F32)
        for yy in range(1, 4):
            total += stack_parts(srecv.at[:, yy], l).astype(F32)
        total = (total * gain_rows(l)).astype(BF16)
        out = (dot_nt(total, wmix[l]) + stack(go, l).astype(F32)).astype(BF16)
        for n, k in enumerate(ks(l)):
            ng[:, cols(k)] = out[n * 16 : (n + 1) * 16]
        wl[l * C : (l + 1) * C, :] = dot_tn(stack(nf, l), total).astype(BF16)

    sibling = g + 1 - 2 * core
    mine = rows(core * HALF, HALF)
    other = rows((1 - core) * HALF, HALF)
    remote(wl.at[other], sibr, send.at[7], sem.at[7], graph=sibling)
    wait(sibr, sem.at[7])
    hb[...] = (wl[mine, :].astype(F32) + sibr[...].astype(F32)).astype(BF16)
    for t in range(1, 8):
        to = lax.rem(chip + t, 8)
        remote(
            hb.at[rows(to * PIECE, PIECE)], grv.at[rows((t - 1) * PIECE, PIECE)], send.at[8], sem.at[8],
            graph=to * 2 + core,
        )
    wait(grv, sem.at[8])
    total = hb[rows(chip * PIECE, PIECE), :].astype(F32)
    for t in range(7):
        total += grv[t * PIECE : (t + 1) * PIECE, :].astype(F32)
    db[:PIECE, :] = total.astype(BF16)
    if dp > 1:
        db[PIECE:, :] = jnp.zeros((8 * TINY - PIECE, C), BF16)
        for t in range(1, dp):
            to = lax.rem(d + t, dp)
            remote(db.at[rows(to * TINY, TINY)], drv.at[rows((t - 1) * TINY, TINY)], send.at[9], sem.at[9], dp=to)
        wait(drv, sem.at[9])
        total = db[rows(d * TINY, TINY), :].astype(F32)
        for t in range(dp - 1):
            total += drv[t * TINY : (t + 1) * TINY, :].astype(F32)
        fin[...] = total.astype(BF16)
        for t in range(1, dp):
            to = lax.rem(d + t, dp)
            remote(fin, ag1.at[rows(d * TINY, TINY)], send.at[10], sem.at[10], dp=to)
        wait(drv, sem.at[10])
        ag1[rows(d * TINY, TINY), :] = fin[...]
    else:
        ag1[...] = db[...]
    for t in range(1, 8):
        to = lax.rem(chip + t, 8)
        remote(
            ag1.at[0:PIECE], ag2.at[rows(chip * PIECE, PIECE)], send.at[11], sem.at[11], graph=to * 2 + core
        )
    wait(grv, sem.at[11])
    ag2[rows(chip * PIECE, PIECE), :] = ag1[:PIECE, :]
    remote(ag2, full.at[mine], send.at[12], sem.at[12], graph=sibling)
    full[mine, :] = ag2[...]
    wait(ag2, sem.at[12])

    for l in range(DEGREES):
        gm[l] = full[l * C : (l + 1) * C, :].astype(F32)
        gw[l] = full[(DEGREES + l) * C : (DEGREES + l + 1) * C, :].astype(F32)
        at_row = 2 * DEGREES * C + l * 512
        gr[:, cols(l)] = full[at_row : at_row + 512, :].astype(F32)

    wait(meta.at[0:240], send.at[0])

    @pl.when(q < 2)
    def _():
        wait(rs.at[0 : 27 * 64], send.at[1])

    @pl.when(q == 2)
    def _():
        wait(rs.at[0 : 26 * 64], send.at[1])

    @pl.when(q == 3)
    def _():
        wait(rs.at[0 : 25 * 64], send.at[1])

    wait(hall.at[0:240], send.at[2])
    wait(dgall.at[0:48], send.at[3])
    wait(ss.at[0:240], send.at[4])
    wait(aggs.at[0:48], send.at[5])
    for n_s, cond in ((1, q < 2), (2, q == 2), (3, q == 3)):
        @pl.when(cond)
        def _():
            wait(drs.at[pl.ds(0, n_s), 0:960], send.at[6])
    wait(sibr, send.at[7])
    wait(grv, send.at[8])
    if dp > 1:
        wait(drv, send.at[9])
        wait(drv, send.at[10])
    wait(grv, send.at[11])
    wait(ag2, send.at[12])


def on_device(dp, node_feat, atomic, edge_src, edge_dst, edge_count, radial, species_gain, w_rad, w_mix, w_out, g_out):
    vmem = pl.BlockSpec(memory_space=pltpu.VMEM)
    scratch = [
        ((4, 16, WPART), BF16),
        ((256, WPART), BF16),
        ((4, 16, WPART), BF16),
        ((128, WPART), BF16),
        ((7 * 256, C), BF16),
        ((3, 1024, C), BF16),
        ((4, 16, C), BF16),
        ((256, C), BF16),
        ((1024, 256), BF16),
        ((256, 1024), BF16),
        ((1024, C), BF16),
        ((C, 1024), BF16),
        ((1024, 5 * C), BF16),
        ((1024, 5 * C), BF16),
        ((3, 1024, C), F32),
        ((3, 1024, C), BF16),
        ((7, 256, C), BF16),
        ((256, WPART), BF16),
        ((4, 4, 16, WPART), BF16),
        ((64, WPART), BF16),
        ((4, 16, WPART), BF16),
        ((256, 512), BF16),
        ((16, DEGREES * C), F32),
        ((ROWS, C), BF16),
        ((HALF, C), BF16),
        ((HALF, C), BF16),
        ((7 * PIECE, C), BF16),
        ((8 * TINY, C), BF16),
        ((7 * TINY, C), BF16),
        ((TINY, C), BF16),
        ((8 * TINY, C), BF16),
        ((HALF, C), BF16),
        ((ROWS, C), BF16),
    ]
    outs = pl.pallas_call(
        functools.partial(kernel, dp),
        out_shape=[
            jax.ShapeDtypeStruct((16, 49 * C), BF16),
            jax.ShapeDtypeStruct((16, 49 * C), BF16),
            jax.ShapeDtypeStruct((256, 512), BF16),
            jax.ShapeDtypeStruct((DEGREES, C, C), F32),
            jax.ShapeDtypeStruct((DEGREES, C, C), F32),
            jax.ShapeDtypeStruct((512, DEGREES * C), F32),
        ],
        in_specs=[vmem] * 11,
        out_specs=[vmem] * 6,
        scratch_shapes=[pltpu.VMEM(s, t) for s, t in scratch]
        + [
            pltpu.SemaphoreType.DMA((len(CHUNKS),)),
            pltpu.SemaphoreType.DMA((len(CHUNKS),)),
            pltpu.SemaphoreType.DMA((13,)),
            pltpu.SemaphoreType.DMA((13,)),
        ],
        compiler_params=pltpu.CompilerParams(
            collective_id=0, has_side_effects=True, vmem_limit_bytes=48 * 1024 * 1024
        ),
    )(
        node_feat[0], atomic, edge_src, edge_dst, edge_count, radial[0], species_gain, w_rad, w_mix, w_out, g_out[0]
    )
    block_out, node_grad, edge_grad, wmix_g, wout_g, wrad_g = outs
    return (block_out[None], node_grad[None], edge_grad[None], wmix_g, wout_g, wrad_g)


def solution(mesh):
    split, whole = P("dp", "graph"), P()
    return jax.shard_map(
        functools.partial(on_device, mesh.shape["dp"]),
        mesh=mesh,
        in_specs=(split, split, split, split, split, split, whole, whole, whole, whole, split),
        out_specs=(split, split, split, whole, whole, whole),
        check_vma=False,
    )
```
